32 devices in a mesh: ex: 4 (over y, x), pb: 8 (over z, core).
Axes of the slice: x: 2, y: 2, z: 4, core: 2. Of those that a mesh axis runs over, the one named last changes fastest.
Arguments:
- train_features: bfloat16 [32768, 4096], P('ex', 'pb'), may hold values from -6 to 6
- query_features: bfloat16 [2048, 4096], P('ex', 'pb'), may hold values from -6 to 6
- precond: bfloat16 [4096, 4096], P('pb'), may hold values from -0.09375 to 0.09375
- example_weight: float32 [32768], P(('ex', 'pb')), may hold values from 0.05 to 0.95
- select: int32 [16, 256], P(None, ('ex', 'pb')), may hold values from 0 to 1, as said below
Outputs:
- scores: float32 [2048, 32768], P(None, ('ex', 'pb'))
The draws below stay inside these ranges and needn't reach their ends.
Inputs may be any that keep to these rules, and one draw needn't show every extreme that they name: `select`: 1 where the pair of query block and training block is to be scored, else 0; the number of listed pairs differs widely between query blocks and between training blocks.
All inputs are finite; a program needn't handle non-finite values.
Results may differ from the reference program's by a relative error of at most 0.0029.
Values may be sent and summed in bfloat16 or wider, within the bound.
A program may use at most 128 MiB of HBM per device.

```python
import jax
import jax.numpy as jnp
from jax import lax

K = 4096
BLK = 128
NQ = 2048
NT = 32768
NQB = 16
NTB = 256


def draw_select(key, part):
    first, second, third = jax.random.split(jax.random.fold_in(key, 17), 3)
    row_level = jax.random.randint(first, (NQB,), 1, 9)
    column_level = jax.random.randint(second, (NTB,), 1, 9)
    rolled = jax.random.randint(third, (NQB, NTB), 0, 64)
    return (rolled < row_level[:, None] * column_level[None, :]).astype(jnp.int32)


def steps_of(own_key, extent, cuts, low, largest):
    gain, own = 1.0, jax.random.fold_in(own_key, 6)
    for position, shards_of in cuts:
        heights = jnp.exp(jax.random.uniform(jax.random.fold_in(own, position), (shards_of,), jnp.float32, low / len(cuts), largest / len(cuts)))
        gain = gain * jnp.repeat(heights, extent[position] // shards_of).reshape([-1 if axis == position else 1 for axis in range(len(extent))])
    return gain


def noise(key, shape, scale, most, cuts=(), dtype=jnp.bfloat16):
    entries = scale * jax.random.normal(key, shape, jnp.float32)
    if cuts:
        entries = entries * steps_of(key, shape, cuts, -0.22, 0.18)
    return jnp.clip(entries, -most, most).astype(dtype)


def setup_inputs(seed: int = 0) -> dict:
    splits = jax.random.split(jax.random.key(seed), 6)
    return {
        "train_features": noise(splits[0], (NT, K), 1.0, 6.0, ((0, 4), (1, 8))),
        "query_features": noise(splits[1], (NQ, K), 1.0, 6.0, ((0, 4), (1, 8))),
        "precond": noise(splits[2], (K, K), K ** -0.5, 0.09375, ((0, 8),)),
        "example_weight": jnp.clip(0.05 + 0.9 * jax.random.uniform(splits[3], (NT,), jnp.float32) ** steps_of(splits[3], (NT,), ((0, 32),), -0.2, 0.2), 0.05, 0.95),
        "select": draw_select(jax.random.fold_in(splits[5], 71), 0),
    }


def reference(train_features, query_features, precond, example_weight, select):
    conditioned = jnp.dot(query_features, precond, preferred_element_type=jnp.float32).astype(jnp.bfloat16)
    raw_scores = lax.dot_general(conditioned, train_features, (((1,), (1,)), ((), ())), preferred_element_type=jnp.float32)
    weighted = raw_scores * (K ** -0.5) * example_weight[None, :]
    keep_mask = select.astype(jnp.float32)
    masked = weighted.reshape(NQB, BLK, NTB, BLK) * keep_mask[:, None, :, None]
    return masked.reshape(NQ, NT)
```

```python
import functools

import jax
import jax.numpy as jnp
from jax import lax
from jax.experimental import pallas as pl
from jax.experimental.pallas import tpu as pltpu
from jax.sharding import PartitionSpec as P

BLK = 128
ROW_TILE = 512


def flip(index, mask):
    bit = 1
    while bit <= mask:
        if mask & bit:
            index = index + bit * (1 - 2 * ((index // bit) % 2))
        bit *= 2
    return index


def bits_of(count):
    return [1 << position for position in range(count.bit_length() - 1)]


def gather_stages(order):
    held, stages = [0], []
    for bit in order:
        stages.append((bit, list(held)))
        held = held + [mask ^ bit for mask in held]
    return stages


def copy_count(ex_count, pb_count):
    return 8 * pb_count + 8 * ex_count


def kernel(ex_count, pb_count, train, query, pre, out, q_all, p_all, c_all, t_all, c_sum, send_sem, recv_sem, local_sem):
    e, p = lax.axis_index("ex"), lax.axis_index("pb")
    core, line = p % 2, p // 2
    rows, width = query.shape
    share = pre.shape[0] // ex_count
    t_rows = t_all.shape[1]
    pb_bits, ex_bits = bits_of(pb_count), bits_of(ex_count)
    top = pb_bits[-1]

    barrier = pltpu.get_barrier_semaphore()
    for mask in range(1, pb_count):
        pl.semaphore_signal(barrier, inc=1, device_id={"pb": flip(p, mask)}, device_id_type=pl.DeviceIdType.MESH)
    for bit in ex_bits:
        pl.semaphore_signal(barrier, inc=1, device_id={"ex": flip(e, bit)}, device_id_type=pl.DeviceIdType.MESH)
    pl.semaphore_wait(barrier, pb_count - 1 + len(ex_bits))

    used = []

    def send(source, target, device):
        number = len(used)
        copy = pltpu.make_async_remote_copy(
            src_ref=source,
            dst_ref=target,
            send_sem=send_sem.at[number],
            recv_sem=recv_sem.at[number],
            device_id=device,
            device_id_type=pl.DeviceIdType.MESH,
        )
        copy.start()
        used.append(copy)
        return copy

    def arrive(copies):
        for copy in copies:
            copy.wait_recv()

    def own(source, target, number):
        copy = pltpu.make_async_copy(source, target, local_sem.at[number])
        copy.start()
        return copy

    def start_train(mask):
        owner = flip(p, mask)
        block = train.at[pl.ds(pl.multiple_of(owner * t_rows, t_rows), t_rows), :]
        return send(block, t_all.at[p], {"pb": owner})

    def start_query(stage):
        bit, held = stage
        copies = []
        for mask in held:
            where = flip(p, mask)
            source = query if mask == 0 else q_all.at[where]
            copies.append(send(source, q_all.at[where], {"pb": flip(p, bit)}))
        return copies

    def pre_part(owner):
        return pre.at[
            pl.ds(pl.multiple_of(e * share, share), share),
            pl.ds(pl.multiple_of(owner * width, width), width),
        ]

    query_stages = gather_stages(pb_bits[::-1])
    pending_q = start_query(query_stages[0])
    pending_p = []
    for mask in range(pb_count - 1, 0, -1):
        owner = flip(p, mask)
        pending_p.append(send(pre_part(owner), p_all.at[p, e], {"pb": owner}))
    local = [
        own(query, q_all.at[p], 0),
        own(pre_part(p), p_all.at[p, e], 1),
        own(train.at[pl.ds(pl.multiple_of(p * t_rows, t_rows), t_rows), :], t_all.at[p], 2),
    ]
    far = list(range(pb_count - 1, top - 1, -1))
    near = list(range(top - 1, 0, -1))
    train_copies = {}
    early = far[: len(far) // 2]
    for mask in early[:1]:
        train_copies[mask] = start_train(mask)
    local[0].wait()
    local[1].wait()
    arrive(pending_q)
    pending_q = start_query(query_stages[1])
    arrive(pending_p)

    half = pb_count // 2
    ex_orders = [ex_bits, ex_bits[1:] + ex_bits[:1]]
    ex_stages = [gather_stages(order) for order in ex_orders]

    q_next = 2
    for step in range(len(ex_bits)):
        pending = []
        for side in range(2):
            bit, held = ex_stages[side][step]
            for mask in held:
                part = p_all.at[pl.ds(side * half, half), flip(e, mask)]
                pending.append(send(part, part, {"ex": flip(e, bit)}))
        if q_next < len(query_stages):
            arrive(pending_q)
            pending_q = start_query(query_stages[q_next])
            q_next += 1
        arrive(pending)
    while q_next < len(query_stages):
        arrive(pending_q)
        pending_q = start_query(query_stages[q_next])
        q_next += 1
    arrive(pending_q)
    for mask in early[1:]:
        train_copies[mask] = start_train(mask)

    c_sum[...] = jnp.zeros_like(c_sum)

    def accumulate(block, carry):
        c_sum[...] += jnp.dot(
            q_all[block],
            p_all[block].reshape(ex_count * share, width),
            preferred_element_type=jnp.float32,
        )
        return carry

    lax.fori_loop(0, pb_count, accumulate, 0)
    own_rows = pl.ds(pl.multiple_of(e * rows, rows), rows)
    c_all[core, line, own_rows, :] = c_sum[...].astype(jnp.bfloat16)

    across = {"pb": flip(p, 1)}
    handed = []
    for bit, held in gather_stages([bit // 2 for bit in pb_bits[:0:-1]]):
        pending = []
        for mask in held:
            part = c_all.at[core, flip(line, mask), own_rows, :]
            pending.append(send(part, part, {"pb": flip(p, 2 * bit)}))
        arrive(pending)
    for mask in far:
        if mask not in train_copies:
            train_copies[mask] = start_train(mask)
    part = c_all.at[core, :, own_rows, :]
    handed.append(send(part, part, across))
    for mask in near:
        train_copies[mask] = start_train(mask)
    side_rows = rows // 2
    for step in range(len(ex_bits)):
        pending, arriving = [], []
        for side in range(2):
            bit, held = ex_stages[side][step]
            for mask in held:
                first = flip(e, mask) * rows + side * side_rows
                part = c_all.at[core, :, pl.ds(pl.multiple_of(first, side_rows), side_rows), :]
                pending.append(send(part, part, {"ex": flip(e, bit)}))
                first = flip(e, mask ^ bit) * rows + side * side_rows
                arriving.append(c_all.at[core, :, pl.ds(pl.multiple_of(first, side_rows), side_rows), :])
        for copy, part in zip(pending, arriving):
            copy.wait_recv()
            handed.append(send(part, part, across))
    arrive(handed)

    for mask in range(pb_count):
        if mask == 0:
            local[2].wait()
        else:
            train_copies[mask].wait_recv()
        block = flip(p, mask)

        def tile(step, carry, block=block, mask=mask):
            at = pl.ds(pl.multiple_of(step * ROW_TILE, ROW_TILE), ROW_TILE)
            product = lax.dot_general(
                c_all[block % 2, block // 2, at, :],
                t_all[block],
                (((1,), (1,)), ((), ())),
                preferred_element_type=jnp.float32,
            )
            if mask == 0:
                out[at, :] = product
            else:
                out[at, :] += product
            return carry

        lax.fori_loop(0, out.shape[0] // ROW_TILE, tile, 0)

    for copy in used:
        copy.wait_send()


def on_device(ex_count, pb_count, train_features, query_features, precond, example_weight, select):
    rows, width = query_features.shape
    t_rows = train_features.shape[0] // pb_count
    queries = rows * ex_count
    share = precond.shape[0] // ex_count
    feature_width = width * pb_count
    copies = copy_count(ex_count, pb_count)
    raw = pl.pallas_call(
        functools.partial(kernel, ex_count, pb_count),
        out_shape=jax.ShapeDtypeStruct((queries, t_rows), jnp.float32),
        in_specs=[pl.BlockSpec(memory_space=pl.ANY)] * 3,
        out_specs=pl.BlockSpec(memory_space=pltpu.VMEM),
        scratch_shapes=[
            pltpu.VMEM((pb_count, rows, width), jnp.bfloat16),
            pltpu.VMEM((pb_count, ex_count, share, width), jnp.bfloat16),
            pltpu.VMEM((2, pb_count // 2, queries, width), jnp.bfloat16),
            pltpu.VMEM((pb_count, t_rows, width), jnp.bfloat16),
            pltpu.VMEM((rows, width), jnp.float32),
            pltpu.SemaphoreType.DMA((copies,)),
            pltpu.SemaphoreType.DMA((copies,)),
            pltpu.SemaphoreType.DMA((3,)),
        ],
        compiler_params=pltpu.CompilerParams(
            collective_id=0, has_side_effects=True, vmem_limit_bytes=56 * 1024 * 1024
        ),
    )(train_features, query_features, precond)
    scaled = raw * feature_width ** (-0.5) * example_weight[None, :]
    keep_mask = select.astype(jnp.float32)
    masked = scaled.reshape(select.shape[0], BLK, select.shape[1], BLK) * keep_mask[:, None, :, None]
    return masked.reshape(raw.shape)


def solution(mesh):
    placed = (P("ex", "pb"), P("ex", "pb"), P("pb", None), P(("ex", "pb")), P(None, ("ex", "pb")))
    return jax.shard_map(
        functools.partial(on_device, mesh.shape["ex"], mesh.shape["pb"]),
        mesh=mesh,
        in_specs=placed,
        out_specs=P(None, ("ex", "pb")),
        check_vma=False,
    )
```

```python
import functools

import jax
import jax.numpy as jnp
from jax import lax
from jax.experimental import pallas as pl
from jax.experimental.pallas import tpu as pltpu
from jax.sharding import PartitionSpec as P

BLK = 128
ROW_TILE = 512
CHUNKS = 4


def flip(index, mask):
    bit = 1
    while bit <= mask:
        if mask & bit:
            index = index + bit * (1 - 2 * ((index // bit) % 2))
        bit *= 2
    return index


def bits_of(count):
    return [1 << position for position in range(count.bit_length() - 1)]


def gather_stages(order):
    held, stages = [0], []
    for bit in order:
        stages.append((bit, list(held)))
        held = held + [mask ^ bit for mask in held]
    return stages


def copy_count(ex_count, pb_count):
    return 8 * pb_count + 8 * ex_count


def kernel(ex_count, pb_count, train, query, pre, factor, out, q_all, p_all, c_all, t_all, c_sum, send_sem, recv_sem, local_sem):
    e, p = lax.axis_index("ex"), lax.axis_index("pb")
    core, line = p % 2, p // 2
    rows, width = query.shape
    share = pre.shape[0] // ex_count
    t_rows = t_all.shape[1]
    pb_bits, ex_bits = bits_of(pb_count), bits_of(ex_count)
    top = pb_bits[-1]

    barrier = pltpu.get_barrier_semaphore()
    for mask in range(1, pb_count):
        pl.semaphore_signal(barrier, inc=1, device_id={"pb": flip(p, mask)}, device_id_type=pl.DeviceIdType.MESH)
    for bit in ex_bits:
        pl.semaphore_signal(barrier, inc=1, device_id={"ex": flip(e, bit)}, device_id_type=pl.DeviceIdType.MESH)
    pl.semaphore_wait(barrier, pb_count - 1 + len(ex_bits))

    used = []

    def send(source, target, device):
        number = len(used)
        copy = pltpu.make_async_remote_copy(
            src_ref=source,
            dst_ref=target,
            send_sem=send_sem.at[number],
            recv_sem=recv_sem.at[number],
            device_id=device,
            device_id_type=pl.DeviceIdType.MESH,
        )
        copy.start()
        used.append(copy)
        return copy

    def arrive(copies):
        for copy in copies:
            copy.wait_recv()

    def own(source, target, number):
        copy = pltpu.make_async_copy(source, target, local_sem.at[number])
        copy.start()
        return copy

    def start_train(mask):
        owner = flip(p, mask)
        block = train.at[pl.ds(pl.multiple_of(owner * t_rows, t_rows), t_rows), :]
        return send(block, t_all.at[p], {"pb": owner})

    def start_query(stage):
        bit, held = stage
        copies = []
        for mask in held:
            where = flip(p, mask)
            source = query if mask == 0 else q_all.at[where]
            copies.append(send(source, q_all.at[where], {"pb": flip(p, bit)}))
        return copies

    def pre_part(owner):
        return pre.at[
            pl.ds(pl.multiple_of(e * share, share), share),
            pl.ds(pl.multiple_of(owner * width, width), width),
        ]

    query_stages = gather_stages(pb_bits[::-1])
    pending_q = start_query(query_stages[0])
    pending_p = []
    for mask in range(pb_count - 1, 0, -1):
        owner = flip(p, mask)
        pending_p.append(send(pre_part(owner), p_all.at[p, e], {"pb": owner}))
    local = [
        own(query, q_all.at[p], 0),
        own(pre_part(p), p_all.at[p, e], 1),
        own(train.at[pl.ds(pl.multiple_of(p * t_rows, t_rows), t_rows), :], t_all.at[p], 2),
    ]
    train_copies = {1: start_train(1)}
    local[0].wait()
    local[1].wait()
    arrive(pending_q)
    pending_q = start_query(query_stages[1])
    arrive(pending_p)
    for mask in [pb_count - 1]:
        train_copies[mask] = start_train(mask)

    half = pb_count // 2
    ex_orders = [ex_bits, ex_bits[1:] + ex_bits[:1]]
    ex_stages = [gather_stages(order) for order in ex_orders]

    q_next = 2
    for step in range(len(ex_bits)):
        pending = []
        for side in range(2):
            bit, held = ex_stages[side][step]
            for mask in held:
                part = p_all.at[pl.ds(side * half, half), flip(e, mask)]
                pending.append(send(part, part, {"ex": flip(e, bit)}))
        if q_next < len(query_stages):
            arrive(pending_q)
            pending_q = start_query(query_stages[q_next])
            q_next += 1
        arrive(pending)
    while q_next < len(query_stages):
        arrive(pending_q)
        pending_q = start_query(query_stages[q_next])
        q_next += 1
    arrive(pending_q)

    across = {"pb": flip(p, 1)}
    chunk_rows = rows // CHUNKS

    def chunk_part(chunk, ex_mask, where):
        first = flip(e, ex_mask) * rows + chunk * chunk_rows
        return c_all.at[core, where, pl.ds(pl.multiple_of(first, chunk_rows), chunk_rows), :]

    line_stages = gather_stages([bit // 2 for bit in pb_bits[:0:-1]])

    def start_line(chunk, stage):
        bit, held = stage
        copies = []
        for mask in held:
            part = chunk_part(chunk, 0, flip(line, mask))
            copies.append(send(part, part, {"pb": flip(p, 2 * bit)}))
        return copies

    def start_ex(chunk, stage):
        bit, held = stage
        copies = []
        for mask in held:
            part = chunk_part(chunk, mask, slice(None))
            copies.append(send(part, part, {"ex": flip(e, bit)}))
        return copies

    handed = []
    pending = {}
    for chunk in range(CHUNKS):
        c_sum[...] = jnp.zeros_like(c_sum)

        def accumulate(block, carry, chunk=chunk):
            c_sum[...] += jnp.dot(
                q_all[block, chunk * chunk_rows : (chunk + 1) * chunk_rows, :],
                p_all[block].reshape(ex_count * share, width),
                preferred_element_type=jnp.float32,
            )
            return carry

        lax.fori_loop(0, pb_count, accumulate, 0)
        first = pl.multiple_of(e * rows + chunk * chunk_rows, chunk_rows)
        c_all[core, line, pl.ds(first, chunk_rows), :] = c_sum[...].astype(jnp.bfloat16)
        pending[chunk] = start_line(chunk, line_stages[0])
    for stage in line_stages[1:]:
        for chunk in range(CHUNKS):
            arrive(pending[chunk])
            pending[chunk] = start_line(chunk, stage)
    for mask in [pb_count - 2]:
        train_copies[mask] = start_train(mask)
    for chunk in range(CHUNKS):
        arrive(pending[chunk])
        pending[chunk] = start_ex(chunk, ex_stages[chunk % 2][0])
        part = chunk_part(chunk, 0, slice(None))
        handed.append(send(part, part, across))
    for mask in range(pb_count - 1, 0, -1):
        if mask not in train_copies:
            train_copies[mask] = start_train(mask)
    for step in range(len(ex_bits)):
        for chunk in range(CHUNKS):
            bit, held = ex_stages[chunk % 2][step]
            arrived = pending[chunk]
            arrive(arrived)
            if step + 1 < len(ex_bits):
                pending[chunk] = start_ex(chunk, ex_stages[chunk % 2][step + 1])
            for mask in held:
                part = chunk_part(chunk, mask ^ bit, slice(None))
                handed.append(send(part, part, across))
    arrive(handed)

    for mask in range(pb_count):
        if mask == 0:
            local[2].wait()
        else:
            train_copies[mask].wait_recv()
        block = flip(p, mask)

        def tile(step, carry, block=block, mask=mask):
            at = pl.ds(pl.multiple_of(step * ROW_TILE, ROW_TILE), ROW_TILE)
            product = lax.dot_general(
                c_all[block % 2, block // 2, at, :],
                t_all[block],
                (((1,), (1,)), ((), ())),
                preferred_element_type=jnp.float32,
            )
            if mask == 0:
                out[at, :] = product
            elif mask < pb_count - 1:
                out[at, :] += product
            else:
                for part in range(ROW_TILE // BLK):
                    here = pl.ds(pl.multiple_of(step * ROW_TILE + part * BLK, BLK), BLK)
                    total = out[here, :] + product[part * BLK : (part + 1) * BLK, :]
                    out[here, :] = total * factor[pl.ds(step * (ROW_TILE // BLK) + part, 1), :]
            return carry

        lax.fori_loop(0, out.shape[0] // ROW_TILE, tile, 0)

    for copy in used:
        copy.wait_send()


def on_device(ex_count, pb_count, train_features, query_features, precond, example_weight, select):
    rows, width = query_features.shape
    t_rows = train_features.shape[0] // pb_count
    queries = rows * ex_count
    share = precond.shape[0] // ex_count
    feature_width = width * pb_count
    copies = copy_count(ex_count, pb_count)
    scale = example_weight * feature_width ** (-0.5)
    factor = jnp.repeat(select.astype(jnp.float32), BLK, axis=1) * scale[None, :]
    return pl.pallas_call(
        functools.partial(kernel, ex_count, pb_count),
        out_shape=jax.ShapeDtypeStruct((queries, t_rows), jnp.float32),
        in_specs=[pl.BlockSpec(memory_space=pl.ANY)] * 3 + [pl.BlockSpec(memory_space=pltpu.VMEM)],
        out_specs=pl.BlockSpec(memory_space=pltpu.VMEM),
        scratch_shapes=[
            pltpu.VMEM((pb_count, rows, width), jnp.bfloat16),
            pltpu.VMEM((pb_count, ex_count, share, width), jnp.bfloat16),
            pltpu.VMEM((2, pb_count // 2, queries, width), jnp.bfloat16),
            pltpu.VMEM((pb_count, t_rows, width), jnp.bfloat16),
            pltpu.VMEM((rows // CHUNKS, width), jnp.float32),
            pltpu.SemaphoreType.DMA((copies,)),
            pltpu.SemaphoreType.DMA((copies,)),
            pltpu.SemaphoreType.DMA((3,)),
        ],
        compiler_params=pltpu.CompilerParams(
            collective_id=0, has_side_effects=True, vmem_limit_bytes=56 * 1024 * 1024
        ),
    )(train_features, query_features, precond, factor)


def solution(mesh):
    placed = (P("ex", "pb"), P("ex", "pb"), P("pb", None), P(("ex", "pb")), P(None, ("ex", "pb")))
    return jax.shard_map(
        functools.partial(on_device, mesh.shape["ex"], mesh.shape["pb"]),
        mesh=mesh,
        in_specs=placed,
        out_specs=P(None, ("ex", "pb")),
        check_vma=False,
    )
```

```python
import functools

import jax
import jax.numpy as jnp
from jax import lax
from jax.experimental import pallas as pl
from jax.experimental.pallas import tpu as pltpu
from jax.sharding import PartitionSpec as P

BLK = 128
ROW_TILE = 512
CHUNKS = 4


def flip(index, mask):
    bit = 1
    while bit <= mask:
        if mask & bit:
            index = index + bit * (1 - 2 * ((index // bit) % 2))
        bit *= 2
    return index


def bits_of(count):
    return [1 << position for position in range(count.bit_length() - 1)]


def gather_stages(order):
    held, stages = [0], []
    for bit in order:
        stages.append((bit, list(held)))
        held = held + [mask ^ bit for mask in held]
    return stages


def copy_count(ex_count, pb_count):
    return 8 * pb_count + 8 * ex_count


def kernel(ex_count, pb_count, train, query, pre, factor, out, q_all, p_all, c_all, t_all, c_sum, send_sem, recv_sem, local_sem):
    e, p = lax.axis_index("ex"), lax.axis_index("pb")
    core, line = p % 2, p // 2
    rows, width = query.shape
    share = pre.shape[0] // ex_count
    t_rows = t_all.shape[1]
    pb_bits, ex_bits = bits_of(pb_count), bits_of(ex_count)
    top = pb_bits[-1]

    barrier = pltpu.get_barrier_semaphore()
    for mask in range(1, pb_count):
        pl.semaphore_signal(barrier, inc=1, device_id={"pb": flip(p, mask)}, device_id_type=pl.DeviceIdType.MESH)
    for bit in ex_bits:
        pl.semaphore_signal(barrier, inc=1, device_id={"ex": flip(e, bit)}, device_id_type=pl.DeviceIdType.MESH)
    pl.semaphore_wait(barrier, pb_count - 1 + len(ex_bits))

    used = []

    def send(source, target, device):
        number = len(used)
        copy = pltpu.make_async_remote_copy(
            src_ref=source,
            dst_ref=target,
            send_sem=send_sem.at[number],
            recv_sem=recv_sem.at[number],
            device_id=device,
            device_id_type=pl.DeviceIdType.MESH,
        )
        copy.start()
        used.append(copy)
        return copy

    def arrive(copies):
        for copy in copies:
            copy.wait_recv()

    def own(source, target, number):
        copy = pltpu.make_async_copy(source, target, local_sem.at[number])
        copy.start()
        return copy

    def start_train(mask):
        owner = flip(p, mask)
        block = train.at[pl.ds(pl.multiple_of(owner * t_rows, t_rows), t_rows), :]
        return send(block, t_all.at[p], {"pb": owner})

    def start_query(stage):
        bit, held = stage
        copies = []
        for mask in held:
            where = flip(p, mask)
            source = query if mask == 0 else q_all.at[where]
            copies.append(send(source, q_all.at[where], {"pb": flip(p, bit)}))
        return copies

    def pre_part(owner):
        return pre.at[
            pl.ds(pl.multiple_of(e * share, share), share),
            pl.ds(pl.multiple_of(owner * width, width), width),
        ]

    query_stages = gather_stages(pb_bits[::-1])
    pending_q = start_query(query_stages[0])
    pending_p = []
    for mask in range(pb_count - 1, 0, -1):
        owner = flip(p, mask)
        pending_p.append(send(pre_part(owner), p_all.at[p, e], {"pb": owner}))
    local = [
        own(query, q_all.at[p], 0),
        own(pre_part(p), p_all.at[p, e], 1),
        own(train.at[pl.ds(pl.multiple_of(p * t_rows, t_rows), t_rows), :], t_all.at[p], 2),
    ]
    train_copies = {1: start_train(1)}
    local[0].wait()
    local[1].wait()
    arrive(pending_q)
    pending_q = start_query(query_stages[1])
    arrive(pending_p)
    for mask in [pb_count - 1]:
        train_copies[mask] = start_train(mask)

    half = pb_count // 2
    ex_orders = [ex_bits, ex_bits[1:] + ex_bits[:1]]
    ex_stages = [gather_stages(order) for order in ex_orders]

    q_next = 2
    for step in range(len(ex_bits)):
        pending = []
        for side in range(2):
            bit, held = ex_stages[side][step]
            for mask in held:
                part = p_all.at[pl.ds(side * half, half), flip(e, mask)]
                pending.append(send(part, part, {"ex": flip(e, bit)}))
        if q_next < len(query_stages):
            arrive(pending_q)
            pending_q = start_query(query_stages[q_next])
            q_next += 1
        arrive(pending)
    while q_next < len(query_stages):
        arrive(pending_q)
        pending_q = start_query(query_stages[q_next])
        q_next += 1
    arrive(pending_q)

    across = {"pb": flip(p, 1)}
    chunk_rows = rows // CHUNKS

    def chunk_part(chunk, ex_mask, where):
        first = flip(e, ex_mask) * rows + chunk * chunk_rows
        return c_all.at[core, where, pl.ds(pl.multiple_of(first, chunk_rows), chunk_rows), :]

    line_stages = gather_stages([bit // 2 for bit in pb_bits[:0:-1]])

    def start_line(chunk, stage):
        bit, held = stage
        copies = []
        for mask in held:
            part = chunk_part(chunk, 0, flip(line, mask))
            copies.append(send(part, part, {"pb": flip(p, 2 * bit)}))
        return copies

    def start_ex(chunk, stage):
        bit, held = stage
        copies = []
        for mask in held:
            part = chunk_part(chunk, mask, slice(None))
            copies.append(send(part, part, {"ex": flip(e, bit)}))
        return copies

    handed = []
    pending = {}
    for chunk in range(CHUNKS):
        c_sum[...] = jnp.zeros_like(c_sum)

        def accumulate(block, carry, chunk=chunk):
            c_sum[...] += jnp.dot(
                q_all[block, chunk * chunk_rows : (chunk + 1) * chunk_rows, :],
                p_all[block].reshape(ex_count * share, width),
                preferred_element_type=jnp.float32,
            )
            return carry

        lax.fori_loop(0, pb_count, accumulate, 0)
        first = pl.multiple_of(e * rows + chunk * chunk_rows, chunk_rows)
        c_all[core, line, pl.ds(first, chunk_rows), :] = c_sum[...].astype(jnp.bfloat16)
        pending[chunk] = start_line(chunk, line_stages[0])
    for stage in line_stages[1:]:
        for chunk in range(CHUNKS):
            arrive(pending[chunk])
            pending[chunk] = start_line(chunk, stage)
    for mask in [pb_count - 2]:
        train_copies[mask] = start_train(mask)
    for chunk in range(CHUNKS):
        arrive(pending[chunk])
        pending[chunk] = start_ex(chunk, ex_stages[chunk % 2][0])
        part = chunk_part(chunk, 0, slice(None))
        handed.append(send(part, part, across))
    for mask in [*range(top - 1, 1, -1), *range(pb_count - 3, top, -1)]:
        train_copies[mask] = start_train(mask)
    for step in range(len(ex_bits)):
        for chunk in range(CHUNKS):
            bit, held = ex_stages[chunk % 2][step]
            arrived = pending[chunk]
            arrive(arrived)
            if step + 1 < len(ex_bits):
                pending[chunk] = start_ex(chunk, ex_stages[chunk % 2][step + 1])
            for mask in held:
                part = chunk_part(chunk, mask ^ bit, slice(None))
                handed.append(send(part, part, across))
    train_copies[top] = start_train(top)
    arrive(handed)

    def product(block, at):
        return lax.dot_general(
            c_all[block % 2, block // 2, at, :],
            t_all[block],
            (((1,), (1,)), ((), ())),
            preferred_element_type=jnp.float32,
        )

    def scores(masks, opening, closing):
        blocks = [flip(p, mask) for mask in masks]

        def tile(step, carry):
            at = pl.ds(pl.multiple_of(step * ROW_TILE, ROW_TILE), ROW_TILE)
            total = product(blocks[0], at)
            for block in blocks[1:]:
                total += product(block, at)
            if opening:
                out[at, :] = total
            elif not closing:
                out[at, :] += total
            else:
                for part in range(ROW_TILE // BLK):
                    here = pl.ds(pl.multiple_of(step * ROW_TILE + part * BLK, BLK), BLK)
                    block_sum = out[here, :] + total[part * BLK : (part + 1) * BLK, :]
                    out[here, :] = block_sum * factor[pl.ds(step * (ROW_TILE // BLK) + part, 1), :]
            return carry

        lax.fori_loop(0, out.shape[0] // ROW_TILE, tile, 0)

    groups = [[*range(top), pb_count - 1], *([mask] for mask in range(pb_count - 2, top - 1, -1))]
    local[2].wait()
    for group in groups:
        for mask in group:
            if mask > 0:
                train_copies[mask].wait_recv()
        scores(group, group is groups[0], group is groups[-1])

    for copy in used:
        copy.wait_send()


def on_device(ex_count, pb_count, train_features, query_features, precond, example_weight, select):
    rows, width = query_features.shape
    t_rows = train_features.shape[0] // pb_count
    queries = rows * ex_count
    share = precond.shape[0] // ex_count
    feature_width = width * pb_count
    copies = copy_count(ex_count, pb_count)
    scale = example_weight * feature_width ** (-0.5)
    factor = jnp.repeat(select.astype(jnp.float32), BLK, axis=1) * scale[None, :]
    return pl.pallas_call(
        functools.partial(kernel, ex_count, pb_count),
        out_shape=jax.ShapeDtypeStruct((queries, t_rows), jnp.float32),
        in_specs=[pl.BlockSpec(memory_space=pl.ANY)] * 3 + [pl.BlockSpec(memory_space=pltpu.VMEM)],
        out_specs=pl.BlockSpec(memory_space=pltpu.VMEM),
        scratch_shapes=[
            pltpu.VMEM((pb_count, rows, width), jnp.bfloat16),
            pltpu.VMEM((pb_count, ex_count, share, width), jnp.bfloat16),
            pltpu.VMEM((2, pb_count // 2, queries, width), jnp.bfloat16),
            pltpu.VMEM((pb_count, t_rows, width), jnp.bfloat16),
            pltpu.VMEM((rows // CHUNKS, width), jnp.float32),
            pltpu.SemaphoreType.DMA((copies,)),
            pltpu.SemaphoreType.DMA((copies,)),
            pltpu.SemaphoreType.DMA((3,)),
        ],
        compiler_params=pltpu.CompilerParams(
            collective_id=0, has_side_effects=True, vmem_limit_bytes=56 * 1024 * 1024
        ),
    )(train_features, query_features, precond, factor)


def solution(mesh):
    placed = (P("ex", "pb"), P("ex", "pb"), P("pb", None), P(("ex", "pb")), P(None, ("ex", "pb")))
    return jax.shard_map(
        functools.partial(on_device, mesh.shape["ex"], mesh.shape["pb"]),
        mesh=mesh,
        in_specs=placed,
        out_specs=P(None, ("ex", "pb")),
        check_vma=False,
    )
```
